32 devices in a mesh: dp: 4 (over z), seq: 4 (over y, x), mp: 2 (over core).
Axes of the slice: x: 2, y: 2, z: 4, core: 2. Of those that a mesh axis runs over, the one named last changes fastest.
Arguments:
- queries: bfloat16 [4, 512, 768], P('dp', 'seq', 'mp'), may hold values from -60 to 60
- keys: bfloat16 [4, 512, 768], P('dp', 'seq', 'mp'), may hold values from -8 to 8
- values: bfloat16 [4, 512, 768], P('dp', 'seq', 'mp'), may hold values from -6 to 6
- proj_weight: bfloat16 [2, 384, 1536], P('mp', 'dp'), may hold values from -0.5 to 0.5
- gate_table: float32 [4, 1536], replicated, may hold values from -6 to 6
- timestep: int32 [4], P('dp'), may hold values from 0 to 3
- span_index: int32 [4], P('dp'), may hold values from 0 to 3
- cotangent: bfloat16 [4, 512, 1536], P('dp', 'seq'), may hold values from -0.0625 to 0.0625
Outputs:
- output: bfloat16 [4, 512, 1536], P('dp', ('seq', 'mp'))
- weight_grad: float32 [2, 4608, 128], P('mp', ('dp', 'seq'))
The draws below stay inside these ranges and needn't reach their ends.
All inputs are finite; a program needn't handle non-finite values.
Results may differ from the reference program's by a relative error of at most 0.015.
Values may be sent and summed in bfloat16 or wider, within the bound.
A program may use at most 64 MiB of HBM per device.

```python
import jax
import jax.numpy as jnp
from jax import lax

D = 1536
HEAD = 128
HEADS = 6
STEPS = 4
TOK_DEV = 128
HD = 768
HDM = 384
ROLLOUTS = 4
SPANS = 4
SEQLEN = 512
GRAD_ROWS = 4608
N_MP = 2


def paired_draw(key):
    base = jax.random.fold_in(key, 11)
    first, second = jax.random.split(base)
    shape = (ROLLOUTS, SEQLEN, HD)
    key_field = 1.5 * jax.random.truncated_normal(first, -4.0, 4.0, shape, jnp.float32)
    query_field = 1.5 * jax.random.truncated_normal(second, -4.0, 4.0, shape, jnp.float32)
    return (query_field, key_field)


def draw_queries(key, part):
    return paired_draw(key)[0].astype(jnp.bfloat16)


def draw_keys(key, part):
    return paired_draw(key)[1].astype(jnp.bfloat16)


def with_ends(array, stream_key, low, top_value):
    longest = array.shape.index(max(array.shape))
    spots = []
    for shift in (0, 1):
        where = [jax.random.randint(jax.random.fold_in(stream_key, axis), (), 0, length) for axis, length in enumerate(array.shape)]
        where[longest] = (where[longest] + shift) % array.shape[longest]
        spots.append(tuple(where))
    return array.at[spots[0]].set(low).at[spots[1]].set(top_value)


def block_levels(stream_key, shape, shards, least, largest):
    gain = 1.0
    for position, blocks in shards:
        draws = jax.random.uniform(jax.random.fold_in(jax.random.fold_in(stream_key, 6), position), (blocks,), jnp.float32, least / len(shards), largest / len(shards))
        gain = gain * jnp.repeat(jnp.exp(draws), shape[position] // blocks).reshape((-1,) + (1,) * (len(shape) - 1 - position))
    return gain


def gaussian(key, shape, spread, bound, shards=(), kind=jnp.bfloat16):
    values = spread * jax.random.normal(key, shape, jnp.float32)
    if shards:
        values = values * block_levels(key, shape, shards, -0.22, 0.18)
    return jnp.clip(values, -bound, bound).astype(kind)


def setup_inputs(seed: int = 0) -> dict:
    arg_keys = jax.random.split(jax.random.key(seed), 9)
    return {
        "queries": draw_queries(jax.random.fold_in(arg_keys[8], 71), 0),
        "keys": draw_keys(jax.random.fold_in(arg_keys[8], 71), 0),
        "values": gaussian(arg_keys[2], (ROLLOUTS, SEQLEN, HD), 1.0, 6.0, ((0, 4), (1, 4), (2, 2))),
        "proj_weight": gaussian(arg_keys[3], (N_MP, HDM, D), HEAD ** -0.5, 0.5, ((0, 2), (1, 4))),
        "gate_table": gaussian(arg_keys[4], (STEPS, D), 1.0, 6.0, (), jnp.float32),
        "timestep": with_ends(jax.random.randint(arg_keys[5], (ROLLOUTS,), 0, STEPS), jax.random.fold_in(arg_keys[5], 1), 0, STEPS - 1).astype(jnp.int32),
        "span_index": with_ends(jax.random.randint(arg_keys[6], (ROLLOUTS,), 0, SPANS), jax.random.fold_in(arg_keys[6], 1), 0, SPANS - 1).astype(jnp.int32),
        "cotangent": gaussian(arg_keys[7], (ROLLOUTS, SEQLEN, D), 0.01, 0.0625, ((0, 4), (1, 4))),
    }


def reference(queries, keys, values, proj_weight, gate_table, timestep, span_index, cotangent):
    inv_root = HEAD ** -0.5
    positions = jnp.arange(SEQLEN, dtype=jnp.int32)
    span_of = positions // TOK_DEV
    weight_full = proj_weight.reshape(HD, D)

    def one_rollout(grad_sum, items):
        query_rows, key_rows, value_rows, step_id, last_span, cot_rows = items
        query_heads = query_rows.reshape(SEQLEN, HEADS, HEAD).astype(jnp.float32)
        key_heads = key_rows.reshape(SEQLEN, HEADS, HEAD).astype(jnp.float32)
        value_heads = value_rows.reshape(SEQLEN, HEADS, HEAD).astype(jnp.float32)
        scores = jnp.einsum('qhd,khd->hqk', query_heads, key_heads) * inv_root
        limit = jnp.minimum(span_of, last_span)
        visible = span_of[None, :] <= limit[:, None]
        scores = jnp.where(visible[None], scores, -jnp.inf)
        row_top = jnp.max(scores, axis=2, keepdims=True)
        weights = jnp.exp(scores - row_top)
        probs = (weights / jnp.sum(weights, axis=2, keepdims=True)).astype(jnp.bfloat16)
        attended = jnp.einsum('hqk,khd->qhd', probs.astype(jnp.float32), value_heads)
        attended = attended.reshape(SEQLEN, HD).astype(jnp.bfloat16)
        mixed = jnp.dot(attended, weight_full, preferred_element_type=jnp.float32)
        gate = gate_table[step_id]
        output = (gate[None, :] * mixed).astype(jnp.bfloat16)
        scaled = (gate[None, :] * cot_rows.astype(jnp.float32)).astype(jnp.bfloat16)
        grad_sum = grad_sum + jnp.dot(attended.T, scaled, preferred_element_type=jnp.float32)
        return grad_sum, output

    start_grad = jnp.zeros((HD, D), jnp.float32)
    grad_sum, output = lax.scan(one_rollout, start_grad, (queries, keys, values, timestep, span_index, cotangent))
    weight_grad = grad_sum.reshape(N_MP, GRAD_ROWS, 128)
    return output, weight_grad
```

```python
import functools

import jax
import jax.numpy as jnp
from jax import lax
from jax.experimental import pallas as pl
from jax.experimental.pallas import tpu as pltpu
from jax.sharding import PartitionSpec as P

HEAD = 128
MESH = pl.DeviceIdType.MESH
PLANE = 4
CHUNKS = 2


def fused(dp_count, q_ref, k_ref, v_ref, w_ref, gate_ref, time_ref, span_ref, cot_ref,
          out_ref, grad_ref,
          kbuf, vbuf, wbuf, cbuf, attn, asend, abuf, gbuf, rsend, rbuf, mix, msend, mrecv, grow,
          local_sem, send_sem, recv_sem):
    tok, width = q_ref.shape
    model = cot_ref.shape[1]
    wrows = w_ref.shape[0]
    wcols = model // PLANE
    half = tok // 2
    piece = width // (dp_count * PLANE)
    part = model // CHUNKS
    heads = width // HEAD
    d, s, m = lax.axis_index("dp"), lax.axis_index("seq"), lax.axis_index("mp")
    x, y = lax.rem(s, 2), s // 2

    def at(mx, my):
        return lax.rem(y + my, 2) * 2 + lax.rem(x + mx, 2)

    first, second, far = at(1 - m, m), at(m, 1 - m), at(1, 1)
    dev = {p: (d, i, m) for p, i in (("a", first), ("b", second), ("c", far))}
    sibling = (d, s, 1 - m)
    depth = [lax.rem(d + o, dp_count) for o in range(dp_count)]
    depth_from = [lax.rem(d + dp_count - o, dp_count) for o in range(dp_count)]

    names = {}
    sent = []

    def remote(name, src, dst, target):
        i = names.setdefault(name, len(names))
        return pltpu.make_async_remote_copy(
            src_ref=src, dst_ref=dst, send_sem=send_sem.at[i], recv_sem=recv_sem.at[i],
            device_id=target, device_id_type=MESH)

    def send(name, src, dst, target):
        copy = remote(name, src, dst, target)
        copy.start()
        sent.append(copy)

    def arrive(name, dst):
        remote(name, dst, dst, sibling).wait_recv()

    def wrow(i):
        return pl.ds(pl.multiple_of(i * wrows, 16), wrows)

    def wcol(i):
        return pl.ds(pl.multiple_of(i * wcols, 128), wcols)

    mine = pl.ds(pl.multiple_of(m * half, 16), half)
    other = pl.ds(pl.multiple_of((1 - m) * half, 16), half)

    local = [
        pltpu.make_async_copy(k_ref, kbuf.at[s], local_sem.at[0]),
        pltpu.make_async_copy(v_ref, vbuf.at[s], local_sem.at[1]),
        pltpu.make_async_copy(cot_ref, cbuf.at[s], local_sem.at[2]),
    ] + [
        pltpu.make_async_copy(
            w_ref.at[:, i * wcols:(i + 1) * wcols], wbuf.at[i, wrow(d)], local_sem.at[3 + i])
        for i in range(PLANE)
    ]

    barrier = pltpu.get_barrier_semaphore()
    partners = [dev["a"], dev["b"], dev["c"], sibling] + [
        (depth[o], s, m) for o in range(1, dp_count)]
    for target in partners:
        pl.semaphore_signal(barrier, inc=1, device_id=target, device_id_type=MESH)
    for copy in local:
        copy.start()
    table = gate_ref[...]
    hit = lax.broadcasted_iota(jnp.int32, table.shape, 0) == time_ref[0]
    grow[...] = jnp.sum(jnp.where(hit, table, 0.0), axis=0, keepdims=True)
    pl.semaphore_wait(barrier, len(partners))

    for p in ("a", "b"):
        send("k" + p, k_ref, kbuf.at[s], dev[p])
        send("v" + p, v_ref, vbuf.at[s], dev[p])
    for o in range(1, dp_count):
        send(f"wz{o}", w_ref.at[:, wcol(s)], wbuf.at[s, wrow(d)], (depth[o], s, m))

    arrive("ka", kbuf.at[first])
    send("kc", kbuf.at[first], kbuf.at[first], dev["b"])
    arrive("va", vbuf.at[first])
    send("vc", vbuf.at[first], vbuf.at[first], dev["b"])
    for p in ("a", "b"):
        send("t" + p, cot_ref.at[mine], cbuf.at[s, mine], dev[p])
    local[0].wait()
    local[1].wait()
    arrive("kb", kbuf.at[second])
    arrive("vb", vbuf.at[second])
    arrive("kc", kbuf.at[far])
    arrive("vc", vbuf.at[far])

    limit = jnp.minimum(s, span_ref[0])
    visible = lax.broadcasted_iota(jnp.int32, (PLANE, tok, tok), 0) <= limit
    columns = []
    for h in range(heads):
        lanes = slice(h * HEAD, (h + 1) * HEAD)
        keys = kbuf[:, :, lanes].reshape(PLANE * tok, HEAD)
        values = vbuf[:, :, lanes].reshape(PLANE * tok, HEAD)
        scores = lax.dot_general(
            keys, q_ref[:, lanes], (((1,), (1,)), ((), ())),
            preferred_element_type=jnp.float32) * (HEAD ** -0.5)
        scores = jnp.where(visible, scores.reshape(PLANE, tok, tok), -jnp.inf)
        scores = scores.reshape(PLANE * tok, tok)
        weights = jnp.exp(scores - jnp.max(scores, axis=0, keepdims=True))
        total = jnp.sum(weights, axis=0, keepdims=True)
        probs = (weights / total).astype(jnp.bfloat16)
        columns.append(lax.dot_general(
            values, probs, (((0,), (0,)), ((), ())), preferred_element_type=jnp.float32))
    turned = jnp.concatenate(columns, axis=0)
    attn[...] = turned.astype(jnp.bfloat16)
    grouped = turned.reshape(dp_count, PLANE, piece, tok)
    for t in range(PLANE):
        asend[t] = grouped[:, t].reshape(dp_count * piece, tok).astype(jnp.bfloat16)
    for p, i in (("c", far), ("a", first), ("b", second)):
        send("o" + p, asend.at[i], abuf.at[s], dev[p])
    abuf[s] = asend[s]

    arrive("ta", cbuf.at[first, mine])
    send("tc", cbuf.at[first, mine], cbuf.at[first, mine], dev["b"])
    send("sa", cbuf.at[first, mine], cbuf.at[first, mine], sibling)
    for o in range(1, dp_count):
        block = wbuf.at[s, wrow(depth_from[o])]
        arrive(f"wz{o}", block)
        for p in ("a", "b"):
            send(f"w{p}{o}", block, block, dev[p])
    arrive("tb", cbuf.at[second, mine])
    send("sb", cbuf.at[second, mine], cbuf.at[second, mine], sibling)

    def project(slot, column):
        mix[slot] = lax.dot_general(
            attn[...], wbuf[column], (((0,), (0,)), ((), ())),
            preferred_element_type=jnp.float32)
        msend[slot] = mix[slot, other].astype(jnp.bfloat16)
        send(f"m{slot}", msend.at[slot], mrecv.at[slot], sibling)

    for copy in local[2:]:
        copy.wait()
    project(0, s)

    arrive("tc", cbuf.at[far, mine])
    send("sc", cbuf.at[far, mine], cbuf.at[far, mine], sibling)
    for p, i in (("c", far), ("a", first), ("b", second)):
        arrive("o" + p, abuf.at[i])
    for p, i in (("a", second), ("b", first), ("c", far)):
        arrive("s" + p, cbuf.at[i, other])

    rows = jnp.concatenate([abuf[j] for j in range(PLANE)], axis=1)
    for c in range(CHUNKS):
        lanes = slice(c * part, (c + 1) * part)
        term = jnp.dot(
            rows, cbuf[:, :, lanes].reshape(PLANE * tok, part),
            preferred_element_type=jnp.float32) * grow[:, lanes]
        term = term.reshape(dp_count, piece, part)
        gbuf[:, :, lanes] = term
        stacked = jnp.concatenate(
            [term[:, :, :part // 2], term[:, :, part // 2:]], axis=1).astype(jnp.bfloat16)
        rsend[c] = stacked
        for o in range(1, dp_count):
            send(f"r{c}{o}", rsend.at[c, depth[o]], rbuf.at[c, o - 1], (depth[o], s, m))

    for o in range(1, dp_count):
        block = wbuf.at[first, wrow(depth_from[o])]
        arrive(f"wa{o}", block)
        send(f"wc{o}", block, block, dev["b"])
    for o in range(1, dp_count):
        arrive(f"wb{o}", wbuf.at[second, wrow(depth_from[o])])
    project(1, at(1, 0))
    project(2, at(0, 1))
    for o in range(1, dp_count):
        arrive(f"wc{o}", wbuf.at[far, wrow(depth_from[o])])
    project(3, far)

    for c in range(CHUNKS):
        lanes = slice(c * part, (c + 1) * part)
        total = gbuf[d, :, lanes]
        for o in range(1, dp_count):
            arrive(f"r{c}{o}", rbuf.at[c, o - 1])
            got = rbuf[c, o - 1].astype(jnp.float32)
            total += jnp.concatenate([got[:piece], got[piece:]], axis=1)
        grad_ref[:, lanes] = total

    for slot, column in enumerate((s, at(1, 0), at(0, 1), far)):
        arrive(f"m{slot}", mrecv.at[slot])
        whole = mix[slot, mine] + mrecv[slot].astype(jnp.float32)
        out_ref[:, wcol(column)] = (grow[:, wcol(column)] * whole).astype(jnp.bfloat16)
    for copy in sent:
        copy.wait_send()


def fused_local(dp_count, queries, keys, values, proj_weight, gate_table, timestep, span_index, cotangent):
    tok, width = queries.shape[1:]
    model = cotangent.shape[2]
    wrows = proj_weight.shape[1]
    piece = width // (dp_count * PLANE)
    bf16, f32 = jnp.bfloat16, jnp.float32
    vmem = pl.BlockSpec(memory_space=pltpu.VMEM)
    smem = pl.BlockSpec(memory_space=pltpu.SMEM)
    anywhere = pl.BlockSpec(memory_space=pl.ANY)
    part = model // CHUNKS
    copies = 16 + 4 + (dp_count - 1) * (4 + CHUNKS)
    output, grad = pl.pallas_call(
        functools.partial(fused, dp_count),
        out_shape=(
            jax.ShapeDtypeStruct((tok // 2, model), bf16),
            jax.ShapeDtypeStruct((piece, model), f32),
        ),
        in_specs=[vmem, anywhere, anywhere, anywhere, vmem, smem, smem, anywhere],
        out_specs=(vmem, vmem),
        scratch_shapes=[
            pltpu.VMEM((PLANE, tok, width), bf16),
            pltpu.VMEM((PLANE, tok, width), bf16),
            pltpu.VMEM((PLANE, dp_count * wrows, model // PLANE), bf16),
            pltpu.VMEM((PLANE, tok, model), bf16),
            pltpu.VMEM((width, tok), bf16),
            pltpu.VMEM((PLANE, dp_count * piece, tok), bf16),
            pltpu.VMEM((PLANE, dp_count * piece, tok), bf16),
            pltpu.VMEM((dp_count, piece, model), f32),
            pltpu.VMEM((CHUNKS, dp_count, 2 * piece, part // 2), bf16),
            pltpu.VMEM((CHUNKS, dp_count - 1, 2 * piece, part // 2), bf16),
            pltpu.VMEM((PLANE, tok, model // PLANE), f32),
            pltpu.VMEM((PLANE, tok // 2, model // PLANE), bf16),
            pltpu.VMEM((PLANE, tok // 2, model // PLANE), bf16),
            pltpu.VMEM((1, model), f32),
            pltpu.SemaphoreType.DMA((3 + PLANE,)),
            pltpu.SemaphoreType.DMA((copies,)),
            pltpu.SemaphoreType.DMA((copies,)),
        ],
        compiler_params=pltpu.CompilerParams(
            collective_id=0, has_side_effects=True, vmem_limit_bytes=48 * 2**20),
    )(queries[0], keys[0], values[0], proj_weight[0], gate_table, timestep, span_index, cotangent[0])
    return output[None], grad.reshape(1, -1, 128)


def local(queries, keys, values, proj_weight, gate_table, timestep, span_index, cotangent):
    tok_rows = queries.shape[1]
    width = queries.shape[2]
    heads_here = width // HEAD
    inv_root = HEAD ** (-0.5)
    seq_place = lax.axis_index("seq")
    all_keys, all_values = (
        lax.all_gather(keys[0], "seq", axis=0, tiled=True),
        lax.all_gather(values[0], "seq", axis=0, tiled=True),
    )
    key_count = all_keys.shape[0]
    query_heads = queries[0].reshape(tok_rows, heads_here, HEAD)
    key_heads = all_keys.reshape(key_count, heads_here, HEAD)
    value_heads = all_values.reshape(key_count, heads_here, HEAD)
    scores = (
        jnp.einsum("qhd,khd->hqk", query_heads, key_heads, preferred_element_type=jnp.float32)
        * inv_root
    )
    key_span = jnp.arange(key_count, dtype=jnp.int32) // tok_rows
    visible = key_span <= jnp.minimum(seq_place, span_index[0])
    scores = jnp.where(visible[None, None, :], scores, -jnp.inf)
    row_top = jnp.max(scores, axis=2, keepdims=True)
    weights = jnp.exp(scores - row_top)
    probs = (weights / jnp.sum(weights, axis=2, keepdims=True)).astype(jnp.bfloat16)
    attended = jnp.einsum("hqk,khd->qhd", probs, value_heads, preferred_element_type=jnp.float32)
    attended = attended.reshape(tok_rows, width).astype(jnp.bfloat16)
    weight_rows = lax.all_gather(proj_weight, "dp", axis=1, tiled=True)
    mixed = jnp.dot(attended, weight_rows[0], preferred_element_type=jnp.float32)
    shared = lax.psum_scatter(
        mixed.astype(jnp.bfloat16), "mp", scatter_dimension=0, tiled=True
    ).astype(jnp.float32)
    step_hit = jnp.arange(gate_table.shape[0], dtype=jnp.int32) == timestep[0]
    gate = jnp.sum(jnp.where(step_hit[:, None], gate_table, 0.0), axis=0)
    output = (gate[None, :] * shared).astype(jnp.bfloat16)[None]
    scaled = (gate[None, :] * cotangent[0].astype(jnp.float32)).astype(jnp.bfloat16)
    term = jnp.dot(attended.T, scaled, preferred_element_type=jnp.float32).reshape(-1, 128)
    rows_all = term.shape[0]
    dp_count = lax.axis_size("dp")
    seq_count = lax.axis_size("seq")
    block_rows = rows_all // (dp_count * seq_count)
    grid_view = term.reshape(dp_count, seq_count, block_rows, 128)
    local_sum = lax.psum_scatter(
        grid_view.transpose(1, 0, 2, 3)
        .reshape(lax.axis_size("seq") * (rows_all // seq_count), 128)
        .astype(jnp.bfloat16),
        "seq",
        scatter_dimension=0,
        tiled=True,
    ).astype(jnp.float32)
    piece = lax.psum_scatter(local_sum, "dp", scatter_dimension=0, tiled=True)
    return (output, piece[None])


def solution(mesh):
    small = mesh.shape["seq"] == PLANE and mesh.shape["mp"] == 2 and mesh.shape["dp"] == 4
    return jax.shard_map(
        functools.partial(fused_local, mesh.shape["dp"]) if small else local,
        mesh=mesh,
        in_specs=(
            P("dp", "seq", "mp"),
            P("dp", "seq", "mp"),
            P("dp", "seq", "mp"),
            P("mp", "dp", None),
            P(),
            P("dp"),
            P("dp"),
            P("dp", "seq", None),
        ),
        out_specs=(P("dp", ("seq", "mp"), None), P("mp", ("dp", "seq"), None)),
        check_vma=False,
    )
```

```python
import functools

import jax
import jax.numpy as jnp
from jax import lax
from jax.experimental import pallas as pl
from jax.experimental.pallas import tpu as pltpu
from jax.sharding import PartitionSpec as P

HEAD = 128
MESH = pl.DeviceIdType.MESH
PLANE = 4
CHUNKS = 2


def fused(dp_count, q_hbm, k_ref, v_ref, w_ref, gate_hbm, time_ref, span_ref, cot_ref,
          out_ref, grad_ref,
          q_ref, gate_ref, kbuf, vbuf, wbuf, cbuf, attn, sbuf, tbuf, asend, abuf, gbuf, rsend, rbuf, mix, msend, mrecv, grow,
          local_sem, send_sem, recv_sem):
    tok, width = q_hbm.shape
    model = cot_ref.shape[1]
    wrows = w_ref.shape[0]
    wcols = model // PLANE
    half = tok // 2
    piece = width // (dp_count * PLANE)
    part = model // CHUNKS
    heads = width // HEAD
    d, s, m = lax.axis_index("dp"), lax.axis_index("seq"), lax.axis_index("mp")
    x, y = lax.rem(s, 2), s // 2

    def at(mx, my):
        return lax.rem(y + my, 2) * 2 + lax.rem(x + mx, 2)

    first, second, far = at(1 - m, m), at(m, 1 - m), at(1, 1)
    dev = {p: (d, i, m) for p, i in (("a", first), ("b", second), ("c", far))}
    sibling = (d, s, 1 - m)
    depth = [lax.rem(d + o, dp_count) for o in range(dp_count)]
    depth_from = [lax.rem(d + dp_count - o, dp_count) for o in range(dp_count)]

    names = {}
    sent = []

    def remote(name, src, dst, target):
        i = names.setdefault(name, len(names))
        return pltpu.make_async_remote_copy(
            src_ref=src, dst_ref=dst, send_sem=send_sem.at[i], recv_sem=recv_sem.at[i],
            device_id=target, device_id_type=MESH)

    def send(name, src, dst, target):
        copy = remote(name, src, dst, target)
        copy.start()
        sent.append(copy)

    def arrive(name, dst):
        remote(name, dst, dst, sibling).wait_recv()

    def wrow(i):
        return pl.ds(pl.multiple_of(i * wrows, 16), wrows)

    def wcol(i):
        return pl.ds(pl.multiple_of(i * wcols, 128), wcols)

    mine = pl.ds(pl.multiple_of(m * half, 16), half)
    other = pl.ds(pl.multiple_of((1 - m) * half, 16), half)

    local = [
        pltpu.make_async_copy(k_ref, kbuf.at[s], local_sem.at[0]),
        pltpu.make_async_copy(v_ref, vbuf.at[s], local_sem.at[1]),
        pltpu.make_async_copy(cot_ref, cbuf.at[s], local_sem.at[2]),
    ] + [
        pltpu.make_async_copy(
            w_ref.at[:, i * wcols:(i + 1) * wcols], wbuf.at[i, wrow(d)], local_sem.at[3 + i])
        for i in range(PLANE)
    ]
    early = [
        pltpu.make_async_copy(gate_hbm, gate_ref, local_sem.at[3 + PLANE]),
        pltpu.make_async_copy(q_hbm, q_ref, local_sem.at[4 + PLANE]),
    ]

    barrier = pltpu.get_barrier_semaphore()
    partners = [dev["a"], dev["b"], dev["c"], sibling] + [
        (depth[o], s, m) for o in range(1, dp_count)]
    for target in partners:
        pl.semaphore_signal(barrier, inc=1, device_id=target, device_id_type=MESH)
    for copy in early + local:
        copy.start()
    pl.semaphore_wait(barrier, len(partners))

    for p in ("a", "b"):
        send("k" + p, k_ref, kbuf.at[s], dev[p])
    for p in ("a", "b"):
        send("v" + p, v_ref, vbuf.at[s], dev[p])
    for o in range(1, dp_count):
        send(f"wz{o}", w_ref.at[:, wcol(s)], wbuf.at[s, wrow(d)], (depth[o], s, m))

    early[0].wait()
    table = gate_ref[...]
    hit = lax.broadcasted_iota(jnp.int32, table.shape, 0) == time_ref[0]
    grow[...] = jnp.sum(jnp.where(hit, table, 0.0), axis=0, keepdims=True)
    limit = jnp.minimum(s, span_ref[0])

    def score(span):
        for h in range(heads):
            lanes = slice(h * HEAD, (h + 1) * HEAD)
            raw = lax.dot_general(
                kbuf[span, :, lanes], q_ref[:, lanes], (((1,), (1,)), ((), ())),
                preferred_element_type=jnp.float32) * (HEAD ** -0.5)
            sbuf[h, span] = jnp.where(jnp.full(raw.shape, span, jnp.int32) <= limit, raw, -jnp.inf)

    def turn(span):
        for h in range(heads):
            lanes = slice(h * HEAD, (h + 1) * HEAD)
            tbuf[h, span] = vbuf[span, :, lanes].T

    early[1].wait()
    local[0].wait()
    score(s)
    local[1].wait()
    turn(s)
    arrive("ka", kbuf.at[first])
    send("kc", kbuf.at[first], kbuf.at[first], dev["b"])
    score(first)
    arrive("va", vbuf.at[first])
    send("vc", vbuf.at[first], vbuf.at[first], dev["b"])
    for p in ("a", "b"):
        send("t" + p, cot_ref.at[mine], cbuf.at[s, mine], dev[p])
    turn(first)
    arrive("kb", kbuf.at[second])
    score(second)
    arrive("vb", vbuf.at[second])
    turn(second)
    arrive("kc", kbuf.at[far])
    score(far)

    probs = []
    for h in range(heads):
        scores = sbuf[h].reshape(PLANE * tok, tok)
        weights = jnp.exp(scores - jnp.max(scores, axis=0, keepdims=True))
        scale = 1.0 / jnp.sum(weights, axis=0, keepdims=True)
        probs.append((weights * scale).astype(jnp.bfloat16))
    arrive("vc", vbuf.at[far])
    turn(far)
    columns = []
    for h in range(heads):
        values = jnp.concatenate([tbuf[h, j] for j in range(PLANE)], axis=1)
        columns.append(jnp.dot(values, probs[h], preferred_element_type=jnp.float32))
    turned = jnp.concatenate(columns, axis=0)
    grouped = turned.reshape(dp_count, PLANE, piece, tok)
    for t in range(PLANE):
        asend[t] = grouped[:, t].reshape(dp_count * piece, tok).astype(jnp.bfloat16)
    for p, i in (("c", far), ("a", first), ("b", second)):
        send("o" + p, asend.at[i], abuf.at[s], dev[p])
    abuf[s] = asend[s]
    attn[...] = turned.T.astype(jnp.bfloat16)

    arrive("ta", cbuf.at[first, mine])
    send("tc", cbuf.at[first, mine], cbuf.at[first, mine], dev["b"])
    send("sa", cbuf.at[first, mine], cbuf.at[first, mine], sibling)
    for o in range(1, dp_count):
        block = wbuf.at[s, wrow(depth_from[o])]
        arrive(f"wz{o}", block)
        for p in ("a", "b"):
            send(f"w{p}{o}", block, block, dev[p])
    arrive("tb", cbuf.at[second, mine])
    send("sb", cbuf.at[second, mine], cbuf.at[second, mine], sibling)

    def project(slot, column):
        mix[slot] = lax.dot_general(
            attn[...], wbuf[column], (((1,), (0,)), ((), ())),
            preferred_element_type=jnp.float32)
        msend[slot] = mix[slot, other].astype(jnp.bfloat16)
        send(f"m{slot}", msend.at[slot], mrecv.at[slot], sibling)

    for copy in local[2:]:
        copy.wait()
    project(0, s)

    arrive("tc", cbuf.at[far, mine])
    send("sc", cbuf.at[far, mine], cbuf.at[far, mine], sibling)
    for p, i in (("c", far), ("a", first), ("b", second)):
        arrive("o" + p, abuf.at[i])
    for p, i in (("a", second), ("b", first), ("c", far)):
        arrive("s" + p, cbuf.at[i, other])

    rows = jnp.concatenate([abuf[j] for j in range(PLANE)], axis=1)
    for c in range(CHUNKS):
        lanes = slice(c * part, (c + 1) * part)
        term = jnp.dot(
            rows, cbuf[:, :, lanes].reshape(PLANE * tok, part),
            preferred_element_type=jnp.float32) * grow[:, lanes]
        term = term.reshape(dp_count, piece, part)
        gbuf[:, :, lanes] = term
        stacked = jnp.concatenate(
            [term[:, :, :part // 2], term[:, :, part // 2:]], axis=1).astype(jnp.bfloat16)
        rsend[c] = stacked
        for o in range(1, dp_count):
            send(f"r{c}{o}", rsend.at[c, depth[o]], rbuf.at[c, o - 1], (depth[o], s, m))

    for o in range(1, dp_count):
        block = wbuf.at[first, wrow(depth_from[o])]
        arrive(f"wa{o}", block)
        send(f"wc{o}", block, block, dev["b"])
    for o in range(1, dp_count):
        arrive(f"wb{o}", wbuf.at[second, wrow(depth_from[o])])
    project(1, at(1, 0))
    project(2, at(0, 1))
    for o in range(1, dp_count):
        arrive(f"wc{o}", wbuf.at[far, wrow(depth_from[o])])
    project(3, far)

    for c in range(CHUNKS):
        lanes = slice(c * part, (c + 1) * part)
        total = gbuf[d, :, lanes]
        for o in range(1, dp_count):
            arrive(f"r{c}{o}", rbuf.at[c, o - 1])
            got = rbuf[c, o - 1].astype(jnp.float32)
            total += jnp.concatenate([got[:piece], got[piece:]], axis=1)
        grad_ref[:, lanes] = total

    for slot, column in enumerate((s, at(1, 0), at(0, 1), far)):
        arrive(f"m{slot}", mrecv.at[slot])
        whole = mix[slot, mine] + mrecv[slot].astype(jnp.float32)
        out_ref[:, wcol(column)] = (grow[:, wcol(column)] * whole).astype(jnp.bfloat16)
    for copy in sent:
        copy.wait_send()


def fused_local(dp_count, queries, keys, values, proj_weight, gate_table, timestep, span_index, cotangent):
    tok, width = queries.shape[1:]
    model = cotangent.shape[2]
    wrows = proj_weight.shape[1]
    piece = width // (dp_count * PLANE)
    bf16, f32 = jnp.bfloat16, jnp.float32
    vmem = pl.BlockSpec(memory_space=pltpu.VMEM)
    smem = pl.BlockSpec(memory_space=pltpu.SMEM)
    anywhere = pl.BlockSpec(memory_space=pl.ANY)
    part = model // CHUNKS
    copies = 16 + 4 + (dp_count - 1) * (4 + CHUNKS)
    output, grad = pl.pallas_call(
        functools.partial(fused, dp_count),
        out_shape=(
            jax.ShapeDtypeStruct((tok // 2, model), bf16),
            jax.ShapeDtypeStruct((piece, model), f32),
        ),
        in_specs=[anywhere] * 5 + [smem, smem, anywhere],
        out_specs=(vmem, vmem),
        scratch_shapes=[
            pltpu.VMEM((tok, width), bf16),
            pltpu.VMEM(gate_table.shape, f32),
            pltpu.VMEM((PLANE, tok, width), bf16),
            pltpu.VMEM((PLANE, tok, width), bf16),
            pltpu.VMEM((PLANE, dp_count * wrows, model // PLANE), bf16),
            pltpu.VMEM((PLANE, tok, model), bf16),
            pltpu.VMEM((tok, width), bf16),
            pltpu.VMEM((width // HEAD, PLANE, tok, tok), f32),
            pltpu.VMEM((width // HEAD, PLANE, HEAD, tok), bf16),
            pltpu.VMEM((PLANE, dp_count * piece, tok), bf16),
            pltpu.VMEM((PLANE, dp_count * piece, tok), bf16),
            pltpu.VMEM((dp_count, piece, model), f32),
            pltpu.VMEM((CHUNKS, dp_count, 2 * piece, part // 2), bf16),
            pltpu.VMEM((CHUNKS, dp_count - 1, 2 * piece, part // 2), bf16),
            pltpu.VMEM((PLANE, tok, model // PLANE), f32),
            pltpu.VMEM((PLANE, tok // 2, model // PLANE), bf16),
            pltpu.VMEM((PLANE, tok // 2, model // PLANE), bf16),
            pltpu.VMEM((1, model), f32),
            pltpu.SemaphoreType.DMA((5 + PLANE,)),
            pltpu.SemaphoreType.DMA((copies,)),
            pltpu.SemaphoreType.DMA((copies,)),
        ],
        compiler_params=pltpu.CompilerParams(
            collective_id=0, has_side_effects=True, vmem_limit_bytes=62 * 2**20),
    )(queries[0], keys[0], values[0], proj_weight[0], gate_table, timestep, span_index, cotangent[0])
    return output[None], grad.reshape(1, -1, 128)


def local(queries, keys, values, proj_weight, gate_table, timestep, span_index, cotangent):
    tok_rows = queries.shape[1]
    width = queries.shape[2]
    heads_here = width // HEAD
    inv_root = HEAD ** (-0.5)
    seq_place = lax.axis_index("seq")
    all_keys, all_values = (
        lax.all_gather(keys[0], "seq", axis=0, tiled=True),
        lax.all_gather(values[0], "seq", axis=0, tiled=True),
    )
    key_count = all_keys.shape[0]
    query_heads = queries[0].reshape(tok_rows, heads_here, HEAD)
    key_heads = all_keys.reshape(key_count, heads_here, HEAD)
    value_heads = all_values.reshape(key_count, heads_here, HEAD)
    scores = (
        jnp.einsum("qhd,khd->hqk", query_heads, key_heads, preferred_element_type=jnp.float32)
        * inv_root
    )
    key_span = jnp.arange(key_count, dtype=jnp.int32) // tok_rows
    visible = key_span <= jnp.minimum(seq_place, span_index[0])
    scores = jnp.where(visible[None, None, :], scores, -jnp.inf)
    row_top = jnp.max(scores, axis=2, keepdims=True)
    weights = jnp.exp(scores - row_top)
    probs = (weights / jnp.sum(weights, axis=2, keepdims=True)).astype(jnp.bfloat16)
    attended = jnp.einsum("hqk,khd->qhd", probs, value_heads, preferred_element_type=jnp.float32)
    attended = attended.reshape(tok_rows, width).astype(jnp.bfloat16)
    weight_rows = lax.all_gather(proj_weight, "dp", axis=1, tiled=True)
    mixed = jnp.dot(attended, weight_rows[0], preferred_element_type=jnp.float32)
    shared = lax.psum_scatter(
        mixed.astype(jnp.bfloat16), "mp", scatter_dimension=0, tiled=True
    ).astype(jnp.float32)
    step_hit = jnp.arange(gate_table.shape[0], dtype=jnp.int32) == timestep[0]
    gate = jnp.sum(jnp.where(step_hit[:, None], gate_table, 0.0), axis=0)
    output = (gate[None, :] * shared).astype(jnp.bfloat16)[None]
    scaled = (gate[None, :] * cotangent[0].astype(jnp.float32)).astype(jnp.bfloat16)
    term = jnp.dot(attended.T, scaled, preferred_element_type=jnp.float32).reshape(-1, 128)
    rows_all = term.shape[0]
    dp_count = lax.axis_size("dp")
    seq_count = lax.axis_size("seq")
    block_rows = rows_all // (dp_count * seq_count)
    grid_view = term.reshape(dp_count, seq_count, block_rows, 128)
    local_sum = lax.psum_scatter(
        grid_view.transpose(1, 0, 2, 3)
        .reshape(lax.axis_size("seq") * (rows_all // seq_count), 128)
        .astype(jnp.bfloat16),
        "seq",
        scatter_dimension=0,
        tiled=True,
    ).astype(jnp.float32)
    piece = lax.psum_scatter(local_sum, "dp", scatter_dimension=0, tiled=True)
    return (output, piece[None])


def solution(mesh):
    small = mesh.shape["seq"] == PLANE and mesh.shape["mp"] == 2 and mesh.shape["dp"] == 4
    return jax.shard_map(
        functools.partial(fused_local, mesh.shape["dp"]) if small else local,
        mesh=mesh,
        in_specs=(
            P("dp", "seq", "mp"),
            P("dp", "seq", "mp"),
            P("dp", "seq", "mp"),
            P("mp", "dp", None),
            P(),
            P("dp"),
            P("dp"),
            P("dp", "seq", None),
        ),
        out_specs=(P("dp", ("seq", "mp"), None), P("mp", ("dp", "seq"), None)),
        check_vma=False,
    )
```

```python
import functools

import jax
import jax.numpy as jnp
from jax import lax
from jax.experimental import pallas as pl
from jax.experimental.pallas import tpu as pltpu
from jax.sharding import PartitionSpec as P

HEAD = 128
MESH = pl.DeviceIdType.MESH
PLANE = 4
CHUNKS = 2


def fused(dp_count, q_hbm, k_ref, v_ref, w_ref, gate_hbm, time_ref, span_ref, cot_ref,
          out_ref, grad_ref,
          q_ref, gate_ref, kbuf, vbuf, wbuf, cbuf, attn, sbuf, tbuf, asend, abuf, gbuf, rsend, rbuf, mix, msend, mrecv, grow,
          local_sem, send_sem, recv_sem):
    tok, width = q_hbm.shape
    model = cot_ref.shape[1]
    wrows = w_ref.shape[0]
    wcols = model // PLANE
    half = tok // 2
    piece = width // (dp_count * PLANE)
    part = model // CHUNKS
    heads = width // HEAD
    d, s, m = lax.axis_index("dp"), lax.axis_index("seq"), lax.axis_index("mp")
    x, y = lax.rem(s, 2), s // 2

    def at(mx, my):
        return lax.rem(y + my, 2) * 2 + lax.rem(x + mx, 2)

    first, second, far = at(1 - m, m), at(m, 1 - m), at(1, 1)
    dev = {p: (d, i, m) for p, i in (("a", first), ("b", second), ("c", far))}
    sibling = (d, s, 1 - m)
    depth = [lax.rem(d + o, dp_count) for o in range(dp_count)]
    depth_from = [lax.rem(d + dp_count - o, dp_count) for o in range(dp_count)]

    names = {}
    sent = []

    def remote(name, src, dst, target):
        i = names.setdefault(name, len(names))
        return pltpu.make_async_remote_copy(
            src_ref=src, dst_ref=dst, send_sem=send_sem.at[i], recv_sem=recv_sem.at[i],
            device_id=target, device_id_type=MESH)

    def send(name, src, dst, target):
        copy = remote(name, src, dst, target)
        copy.start()
        sent.append(copy)

    def arrive(name, dst):
        remote(name, dst, dst, sibling).wait_recv()

    def wrow(i):
        return pl.ds(pl.multiple_of(i * wrows, 16), wrows)

    def wcol(i):
        return pl.ds(pl.multiple_of(i * wcols, 128), wcols)

    mine = pl.ds(pl.multiple_of(m * half, 16), half)
    other = pl.ds(pl.multiple_of((1 - m) * half, 16), half)

    local = [
        pltpu.make_async_copy(k_ref, kbuf.at[s], local_sem.at[0]),
        pltpu.make_async_copy(v_ref, vbuf.at[s], local_sem.at[1]),
        pltpu.make_async_copy(cot_ref, cbuf.at[s], local_sem.at[2]),
    ] + [
        pltpu.make_async_copy(
            w_ref.at[:, i * wcols:(i + 1) * wcols], wbuf.at[i, wrow(d)], local_sem.at[3 + i])
        for i in range(PLANE)
    ]
    early = [
        pltpu.make_async_copy(gate_hbm, gate_ref, local_sem.at[3 + PLANE]),
        pltpu.make_async_copy(q_hbm, q_ref, local_sem.at[4 + PLANE]),
    ]

    barrier = pltpu.get_barrier_semaphore()
    partners = [dev["a"], dev["b"], dev["c"], sibling] + [
        (depth[o], s, m) for o in range(1, dp_count)]
    for target in partners:
        pl.semaphore_signal(barrier, inc=1, device_id=target, device_id_type=MESH)
    for copy in early + local:
        copy.start()
    pl.semaphore_wait(barrier, len(partners))

    for p in ("a", "b"):
        send("k" + p, k_ref, kbuf.at[s], dev[p])
    for p in ("a", "b"):
        send("v" + p, v_ref, vbuf.at[s], dev[p])
    for o in range(1, dp_count):
        send(f"wz{o}", w_ref.at[:, wcol(s)], wbuf.at[s, wrow(d)], (depth[o], s, m))

    early[0].wait()
    table = gate_ref[...]
    hit = lax.broadcasted_iota(jnp.int32, table.shape, 0) == time_ref[0]
    grow[...] = jnp.sum(jnp.where(hit, table, 0.0), axis=0, keepdims=True)
    limit = jnp.minimum(s, span_ref[0])

    def score(span):
        for h in range(heads):
            lanes = slice(h * HEAD, (h + 1) * HEAD)
            raw = lax.dot_general(
                kbuf[span, :, lanes], q_ref[:, lanes], (((1,), (1,)), ((), ())),
                preferred_element_type=jnp.float32) * (HEAD ** -0.5)
            sbuf[h, span] = jnp.where(jnp.full(raw.shape, span, jnp.int32) <= limit, raw, -jnp.inf)

    def turn(span):
        for h in range(heads):
            lanes = slice(h * HEAD, (h + 1) * HEAD)
            tbuf[h, span] = vbuf[span, :, lanes].T

    early[1].wait()
    local[0].wait()
    score(s)
    local[1].wait()
    turn(s)
    arrive("ka", kbuf.at[first])
    send("kc", kbuf.at[first], kbuf.at[first], dev["b"])
    score(first)
    arrive("va", vbuf.at[first])
    send("vc", vbuf.at[first], vbuf.at[first], dev["b"])
    for p in ("a", "b"):
        send("t" + p, cot_ref.at[mine], cbuf.at[s, mine], dev[p])
    turn(first)
    arrive("kb", kbuf.at[second])
    score(second)
    arrive("vb", vbuf.at[second])
    turn(second)
    arrive("kc", kbuf.at[far])
    score(far)

    probs = []
    for h in range(heads):
        scores = sbuf[h].reshape(PLANE * tok, tok)
        weights = jnp.exp(scores - jnp.max(scores, axis=0, keepdims=True))
        scale = 1.0 / jnp.sum(weights, axis=0, keepdims=True)
        probs.append((weights * scale).astype(jnp.bfloat16))
    arrive("vc", vbuf.at[far])
    turn(far)
    columns = []
    for h in range(heads):
        values = jnp.concatenate([tbuf[h, j] for j in range(PLANE)], axis=1)
        columns.append(jnp.dot(values, probs[h], preferred_element_type=jnp.float32))
    turned = jnp.concatenate(columns, axis=0)
    grouped = turned.reshape(dp_count, PLANE, piece, tok)
    for t in range(PLANE):
        asend[t] = grouped[:, t].reshape(dp_count * piece, tok).astype(jnp.bfloat16)
    for p, i in (("c", far), ("a", first), ("b", second)):
        send("o" + p, asend.at[i], abuf.at[s], dev[p])
    abuf[s] = asend[s]
    attn[...] = turned.T.astype(jnp.bfloat16)

    arrive("ta", cbuf.at[first, mine])
    send("tc", cbuf.at[first, mine], cbuf.at[first, mine], dev["b"])
    send("sa", cbuf.at[first, mine], cbuf.at[first, mine], sibling)
    for o in range(1, dp_count):
        block = wbuf.at[s, wrow(depth_from[o])]
        arrive(f"wz{o}", block)
        for p in ("a", "b"):
            send(f"w{p}{o}", block, block, dev[p])
    arrive("tb", cbuf.at[second, mine])
    send("sb", cbuf.at[second, mine], cbuf.at[second, mine], sibling)

    def project(slot, column):
        mix[slot] = lax.dot_general(
            attn[...], wbuf[column], (((1,), (0,)), ((), ())),
            preferred_element_type=jnp.float32)
        msend[slot] = mix[slot, other].astype(jnp.bfloat16)
        send(f"m{slot}", msend.at[slot], mrecv.at[slot], sibling)

    arrive("tc", cbuf.at[far, mine])
    send("sc", cbuf.at[far, mine], cbuf.at[far, mine], sibling)
    for copy in local[2:]:
        copy.wait()
    project(0, s)
    for p, i in (("c", far), ("a", first), ("b", second)):
        arrive("o" + p, abuf.at[i])
    for p, i in (("a", second), ("b", first), ("c", far)):
        arrive("s" + p, cbuf.at[i, other])

    rows = jnp.concatenate([abuf[j] for j in range(PLANE)], axis=1)
    for c in range(CHUNKS):
        lanes = slice(c * part, (c + 1) * part)
        term = jnp.dot(
            rows, cbuf[:, :, lanes].reshape(PLANE * tok, part),
            preferred_element_type=jnp.float32) * grow[:, lanes]
        term = term.reshape(dp_count, piece, part)
        gbuf[:, :, lanes] = term
        stacked = jnp.concatenate(
            [term[:, :, :part // 2], term[:, :, part // 2:]], axis=1).astype(jnp.bfloat16)
        rsend[c] = stacked
        for o in range(1, dp_count):
            send(f"r{c}{o}", rsend.at[c, depth[o]], rbuf.at[c, o - 1], (depth[o], s, m))

    for o in range(1, dp_count):
        block = wbuf.at[first, wrow(depth_from[o])]
        arrive(f"wa{o}", block)
        send(f"wc{o}", block, block, dev["b"])
    for o in range(1, dp_count):
        arrive(f"wb{o}", wbuf.at[second, wrow(depth_from[o])])
    project(1, at(1, 0))
    project(2, at(0, 1))
    for o in range(1, dp_count):
        arrive(f"wc{o}", wbuf.at[far, wrow(depth_from[o])])
    project(3, far)

    for c in range(CHUNKS):
        lanes = slice(c * part, (c + 1) * part)
        total = gbuf[d, :, lanes]
        for o in range(1, dp_count):
            arrive(f"r{c}{o}", rbuf.at[c, o - 1])
            got = rbuf[c, o - 1].astype(jnp.float32)
            total += jnp.concatenate([got[:piece], got[piece:]], axis=1)
        grad_ref[:, lanes] = total

    for slot, column in enumerate((s, at(1, 0), at(0, 1), far)):
        arrive(f"m{slot}", mrecv.at[slot])
        whole = mix[slot, mine] + mrecv[slot].astype(jnp.float32)
        out_ref[:, wcol(column)] = (grow[:, wcol(column)] * whole).astype(jnp.bfloat16)
    for copy in sent:
        copy.wait_send()


def fused_local(dp_count, queries, keys, values, proj_weight, gate_table, timestep, span_index, cotangent):
    tok, width = queries.shape[1:]
    model = cotangent.shape[2]
    wrows = proj_weight.shape[1]
    piece = width // (dp_count * PLANE)
    bf16, f32 = jnp.bfloat16, jnp.float32
    vmem = pl.BlockSpec(memory_space=pltpu.VMEM)
    smem = pl.BlockSpec(memory_space=pltpu.SMEM)
    anywhere = pl.BlockSpec(memory_space=pl.ANY)
    part = model // CHUNKS
    copies = 16 + 4 + (dp_count - 1) * (4 + CHUNKS)
    output, grad = pl.pallas_call(
        functools.partial(fused, dp_count),
        out_shape=(
            jax.ShapeDtypeStruct((tok // 2, model), bf16),
            jax.ShapeDtypeStruct((piece, model), f32),
        ),
        in_specs=[anywhere] * 5 + [smem, smem, anywhere],
        out_specs=(vmem, vmem),
        scratch_shapes=[
            pltpu.VMEM((tok, width), bf16),
            pltpu.VMEM(gate_table.shape, f32),
            pltpu.VMEM((PLANE, tok, width), bf16),
            pltpu.VMEM((PLANE, tok, width), bf16),
            pltpu.VMEM((PLANE, dp_count * wrows, model // PLANE), bf16),
            pltpu.VMEM((PLANE, tok, model), bf16),
            pltpu.VMEM((tok, width), bf16),
            pltpu.VMEM((width // HEAD, PLANE, tok, tok), f32),
            pltpu.VMEM((width // HEAD, PLANE, HEAD, tok), bf16),
            pltpu.VMEM((PLANE, dp_count * piece, tok), bf16),
            pltpu.VMEM((PLANE, dp_count * piece, tok), bf16),
            pltpu.VMEM((dp_count, piece, model), f32),
            pltpu.VMEM((CHUNKS, dp_count, 2 * piece, part // 2), bf16),
            pltpu.VMEM((CHUNKS, dp_count - 1, 2 * piece, part // 2), bf16),
            pltpu.VMEM((PLANE, tok, model // PLANE), f32),
            pltpu.VMEM((PLANE, tok // 2, model // PLANE), bf16),
            pltpu.VMEM((PLANE, tok // 2, model // PLANE), bf16),
            pltpu.VMEM((1, model), f32),
            pltpu.SemaphoreType.DMA((5 + PLANE,)),
            pltpu.SemaphoreType.DMA((copies,)),
            pltpu.SemaphoreType.DMA((copies,)),
        ],
        compiler_params=pltpu.CompilerParams(
            collective_id=0, has_side_effects=True, vmem_limit_bytes=62 * 2**20),
    )(queries[0], keys[0], values[0], proj_weight[0], gate_table, timestep, span_index, cotangent[0])
    return output[None], grad.reshape(1, -1, 128)


def local(queries, keys, values, proj_weight, gate_table, timestep, span_index, cotangent):
    tok_rows = queries.shape[1]
    width = queries.shape[2]
    heads_here = width // HEAD
    inv_root = HEAD ** (-0.5)
    seq_place = lax.axis_index("seq")
    all_keys, all_values = (
        lax.all_gather(keys[0], "seq", axis=0, tiled=True),
        lax.all_gather(values[0], "seq", axis=0, tiled=True),
    )
    key_count = all_keys.shape[0]
    query_heads = queries[0].reshape(tok_rows, heads_here, HEAD)
    key_heads = all_keys.reshape(key_count, heads_here, HEAD)
    value_heads = all_values.reshape(key_count, heads_here, HEAD)
    scores = (
        jnp.einsum("qhd,khd->hqk", query_heads, key_heads, preferred_element_type=jnp.float32)
        * inv_root
    )
    key_span = jnp.arange(key_count, dtype=jnp.int32) // tok_rows
    visible = key_span <= jnp.minimum(seq_place, span_index[0])
    scores = jnp.where(visible[None, None, :], scores, -jnp.inf)
    row_top = jnp.max(scores, axis=2, keepdims=True)
    weights = jnp.exp(scores - row_top)
    probs = (weights / jnp.sum(weights, axis=2, keepdims=True)).astype(jnp.bfloat16)
    attended = jnp.einsum("hqk,khd->qhd", probs, value_heads, preferred_element_type=jnp.float32)
    attended = attended.reshape(tok_rows, width).astype(jnp.bfloat16)
    weight_rows = lax.all_gather(proj_weight, "dp", axis=1, tiled=True)
    mixed = jnp.dot(attended, weight_rows[0], preferred_element_type=jnp.float32)
    shared = lax.psum_scatter(
        mixed.astype(jnp.bfloat16), "mp", scatter_dimension=0, tiled=True
    ).astype(jnp.float32)
    step_hit = jnp.arange(gate_table.shape[0], dtype=jnp.int32) == timestep[0]
    gate = jnp.sum(jnp.where(step_hit[:, None], gate_table, 0.0), axis=0)
    output = (gate[None, :] * shared).astype(jnp.bfloat16)[None]
    scaled = (gate[None, :] * cotangent[0].astype(jnp.float32)).astype(jnp.bfloat16)
    term = jnp.dot(attended.T, scaled, preferred_element_type=jnp.float32).reshape(-1, 128)
    rows_all = term.shape[0]
    dp_count = lax.axis_size("dp")
    seq_count = lax.axis_size("seq")
    block_rows = rows_all // (dp_count * seq_count)
    grid_view = term.reshape(dp_count, seq_count, block_rows, 128)
    local_sum = lax.psum_scatter(
        grid_view.transpose(1, 0, 2, 3)
        .reshape(lax.axis_size("seq") * (rows_all // seq_count), 128)
        .astype(jnp.bfloat16),
        "seq",
        scatter_dimension=0,
        tiled=True,
    ).astype(jnp.float32)
    piece = lax.psum_scatter(local_sum, "dp", scatter_dimension=0, tiled=True)
    return (output, piece[None])


def solution(mesh):
    small = mesh.shape["seq"] == PLANE and mesh.shape["mp"] == 2 and mesh.shape["dp"] == 4
    return jax.shard_map(
        functools.partial(fused_local, mesh.shape["dp"]) if small else local,
        mesh=mesh,
        in_specs=(
            P("dp", "seq", "mp"),
            P("dp", "seq", "mp"),
            P("dp", "seq", "mp"),
            P("mp", "dp", None),
            P(),
            P("dp"),
            P("dp"),
            P("dp", "seq", None),
        ),
        out_specs=(P("dp", ("seq", "mp"), None), P("mp", ("dp", "seq"), None)),
        check_vma=False,
    )
```

```python
import functools

import jax
import jax.numpy as jnp
from jax import lax
from jax.experimental import pallas as pl
from jax.experimental.pallas import tpu as pltpu
from jax.sharding import PartitionSpec as P

HEAD = 128
MESH = pl.DeviceIdType.MESH
PLANE = 4
CHUNKS = 2


def fused(dp_count, q_hbm, k_ref, v_ref, w_ref, gate_hbm, time_ref, span_ref, cot_ref,
          out_ref, grad_ref,
          q_ref, gate_ref, kbuf, vbuf, wbuf, cbuf, attn, sbuf, tbuf, asend, abuf, gbuf, rsend, rbuf, mix, msend, mrecv, grow,
          local_sem, send_sem, recv_sem):
    tok, width = q_hbm.shape
    model = cot_ref.shape[1]
    wrows = w_ref.shape[0]
    wcols = model // PLANE
    half = tok // 2
    piece = width // (dp_count * PLANE)
    part = model // CHUNKS
    heads = width // HEAD
    d, s, m = lax.axis_index("dp"), lax.axis_index("seq"), lax.axis_index("mp")
    x, y = lax.rem(s, 2), s // 2

    def at(mx, my):
        return lax.rem(y + my, 2) * 2 + lax.rem(x + mx, 2)

    first, second, far = at(1 - m, m), at(m, 1 - m), at(1, 1)
    dev = {p: (d, i, m) for p, i in (("a", first), ("b", second), ("c", far))}
    sibling = (d, s, 1 - m)
    own = 2 * lax.rem(x + y, 2)
    rest = 2 - own
    beside = ((d, at(1, 0), m), (d, at(0, 1), m))
    depth = [lax.rem(d + o, dp_count) for o in range(dp_count)]
    depth_from = [lax.rem(d + dp_count - o, dp_count) for o in range(dp_count)]

    names = {}
    sent = []

    def remote(name, src, dst, target):
        i = names.setdefault(name, len(names))
        return pltpu.make_async_remote_copy(
            src_ref=src, dst_ref=dst, send_sem=send_sem.at[i], recv_sem=recv_sem.at[i],
            device_id=target, device_id_type=MESH)

    def send(name, src, dst, target):
        copy = remote(name, src, dst, target)
        copy.start()
        sent.append(copy)

    def arrive(name, dst):
        remote(name, dst, dst, sibling).wait_recv()

    def wrow(i):
        return pl.ds(pl.multiple_of(i * wrows, 16), wrows)

    def wcol(i):
        return pl.ds(pl.multiple_of(i * wcols, 128), wcols)

    mine = pl.ds(pl.multiple_of(m * half, 16), half)
    other = pl.ds(pl.multiple_of((1 - m) * half, 16), half)

    local = [
        pltpu.make_async_copy(k_ref, kbuf.at[s], local_sem.at[0]),
        pltpu.make_async_copy(v_ref, vbuf.at[s], local_sem.at[1]),
        pltpu.make_async_copy(cot_ref, cbuf.at[s], local_sem.at[2]),
    ] + [
        pltpu.make_async_copy(
            w_ref.at[:, i * wcols:(i + 1) * wcols], wbuf.at[i, wrow(d)], local_sem.at[3 + i])
        for i in range(PLANE)
    ]
    early = [
        pltpu.make_async_copy(gate_hbm, gate_ref, local_sem.at[3 + PLANE]),
        pltpu.make_async_copy(q_hbm, q_ref, local_sem.at[4 + PLANE]),
    ]

    barrier = pltpu.get_barrier_semaphore()
    partners = [dev["a"], dev["b"], dev["c"], sibling] + [
        (depth[o], s, m) for o in range(1, dp_count)]
    for target in partners:
        pl.semaphore_signal(barrier, inc=1, device_id=target, device_id_type=MESH)
    for copy in early + local:
        copy.start()
    pl.semaphore_wait(barrier, len(partners))

    for p in ("a", "b"):
        send("k" + p, k_ref, kbuf.at[s], dev[p])
    for p in ("a", "b"):
        send("v" + p, v_ref, vbuf.at[s], dev[p])
    for o in range(1, dp_count):
        for j in range(2):
            send(f"wz{j}{o}", w_ref.at[:, wcol(own + j)], wbuf.at[own + j, wrow(d)],
                 (depth[o], s, m))

    early[0].wait()
    table = gate_ref[...]
    hit = lax.broadcasted_iota(jnp.int32, table.shape, 0) == time_ref[0]
    grow[...] = jnp.sum(jnp.where(hit, table, 0.0), axis=0, keepdims=True)
    limit = jnp.minimum(s, span_ref[0])

    def score(span):
        for h in range(heads):
            lanes = slice(h * HEAD, (h + 1) * HEAD)
            raw = lax.dot_general(
                kbuf[span, :, lanes], q_ref[:, lanes], (((1,), (1,)), ((), ())),
                preferred_element_type=jnp.float32) * (HEAD ** -0.5)
            sbuf[h, span] = jnp.where(jnp.full(raw.shape, span, jnp.int32) <= limit, raw, -jnp.inf)

    def turn(span):
        for h in range(heads):
            lanes = slice(h * HEAD, (h + 1) * HEAD)
            tbuf[h, span] = vbuf[span, :, lanes].T

    early[1].wait()
    local[0].wait()
    score(s)
    local[1].wait()
    turn(s)
    arrive("ka", kbuf.at[first])
    send("kc", kbuf.at[first], kbuf.at[first], dev["b"])
    score(first)
    arrive("va", vbuf.at[first])
    send("vc", vbuf.at[first], vbuf.at[first], dev["b"])
    for p in ("a", "b"):
        send("t" + p, cot_ref.at[mine], cbuf.at[s, mine], dev[p])
    turn(first)
    arrive("kb", kbuf.at[second])
    score(second)
    arrive("vb", vbuf.at[second])
    turn(second)
    arrive("kc", kbuf.at[far])
    score(far)

    probs = []
    for h in range(heads):
        scores = sbuf[h].reshape(PLANE * tok, tok)
        weights = jnp.exp(scores - jnp.max(scores, axis=0, keepdims=True))
        scale = 1.0 / jnp.sum(weights, axis=0, keepdims=True)
        probs.append((weights * scale).astype(jnp.bfloat16))
    arrive("vc", vbuf.at[far])
    turn(far)
    columns = []
    for h in range(heads):
        values = jnp.concatenate([tbuf[h, j] for j in range(PLANE)], axis=1)
        columns.append(jnp.dot(values, probs[h], preferred_element_type=jnp.float32))
    turned = jnp.concatenate(columns, axis=0)
    grouped = turned.reshape(dp_count, PLANE, piece, tok)
    for t in range(PLANE):
        asend[t] = grouped[:, t].reshape(dp_count * piece, tok).astype(jnp.bfloat16)
    for p, i in (("c", far), ("a", first), ("b", second)):
        send("o" + p, asend.at[i], abuf.at[s], dev[p])
    abuf[s] = asend[s]
    attn[...] = turned.T.astype(jnp.bfloat16)

    arrive("ta", cbuf.at[first, mine])
    send("tc", cbuf.at[first, mine], cbuf.at[first, mine], dev["b"])
    send("sa", cbuf.at[first, mine], cbuf.at[first, mine], sibling)
    arrive("tb", cbuf.at[second, mine])
    send("sb", cbuf.at[second, mine], cbuf.at[second, mine], sibling)

    def project(slot, column):
        mix[slot] = lax.dot_general(
            attn[...], wbuf[column], (((1,), (0,)), ((), ())),
            preferred_element_type=jnp.float32)
        msend[slot] = mix[slot, other].astype(jnp.bfloat16)
        send(f"m{slot}", msend.at[slot], mrecv.at[slot], sibling)

    arrive("tc", cbuf.at[far, mine])
    send("sc", cbuf.at[far, mine], cbuf.at[far, mine], sibling)
    for j in range(2):
        for o in range(1, dp_count):
            block = wbuf.at[own + j, wrow(depth_from[o])]
            arrive(f"wz{j}{o}", block)
            send(f"wn{j}{o}", block, block, beside[j])
    for copy in local[2:]:
        copy.wait()
    project(0, own)
    for p, i in (("c", far), ("a", first), ("b", second)):
        arrive("o" + p, abuf.at[i])
    for p, i in (("a", second), ("b", first), ("c", far)):
        arrive("s" + p, cbuf.at[i, other])

    rows = jnp.concatenate([abuf[j] for j in range(PLANE)], axis=1)
    for c in range(CHUNKS):
        lanes = slice(c * part, (c + 1) * part)
        term = jnp.dot(
            rows, cbuf[:, :, lanes].reshape(PLANE * tok, part),
            preferred_element_type=jnp.float32) * grow[:, lanes]
        term = term.reshape(dp_count, piece, part)
        gbuf[:, :, lanes] = term
        stacked = jnp.concatenate(
            [term[:, :, :part // 2], term[:, :, part // 2:]], axis=1).astype(jnp.bfloat16)
        rsend[c] = stacked
        for o in range(1, dp_count):
            send(f"r{c}{o}", rsend.at[c, depth[o]], rbuf.at[c, o - 1], (depth[o], s, m))

    project(1, own + 1)
    for j in range(2):
        for o in range(1, dp_count):
            arrive(f"wn{j}{o}", wbuf.at[rest + j, wrow(depth_from[o])])
        project(2 + j, rest + j)

    for c in range(CHUNKS):
        lanes = slice(c * part, (c + 1) * part)
        total = gbuf[d, :, lanes]
        for o in range(1, dp_count):
            arrive(f"r{c}{o}", rbuf.at[c, o - 1])
            got = rbuf[c, o - 1].astype(jnp.float32)
            total += jnp.concatenate([got[:piece], got[piece:]], axis=1)
        grad_ref[:, lanes] = total

    for slot, column in enumerate((own, own + 1, rest, rest + 1)):
        arrive(f"m{slot}", mrecv.at[slot])
        whole = mix[slot, mine] + mrecv[slot].astype(jnp.float32)
        out_ref[:, wcol(column)] = (grow[:, wcol(column)] * whole).astype(jnp.bfloat16)
    for copy in sent:
        copy.wait_send()


def fused_local(dp_count, queries, keys, values, proj_weight, gate_table, timestep, span_index, cotangent):
    tok, width = queries.shape[1:]
    model = cotangent.shape[2]
    wrows = proj_weight.shape[1]
    piece = width // (dp_count * PLANE)
    bf16, f32 = jnp.bfloat16, jnp.float32
    vmem = pl.BlockSpec(memory_space=pltpu.VMEM)
    smem = pl.BlockSpec(memory_space=pltpu.SMEM)
    anywhere = pl.BlockSpec(memory_space=pl.ANY)
    part = model // CHUNKS
    copies = 16 + 4 + (dp_count - 1) * (4 + CHUNKS)
    output, grad = pl.pallas_call(
        functools.partial(fused, dp_count),
        out_shape=(
            jax.ShapeDtypeStruct((tok // 2, model), bf16),
            jax.ShapeDtypeStruct((piece, model), f32),
        ),
        in_specs=[anywhere] * 5 + [smem, smem, anywhere],
        out_specs=(vmem, vmem),
        scratch_shapes=[
            pltpu.VMEM((tok, width), bf16),
            pltpu.VMEM(gate_table.shape, f32),
            pltpu.VMEM((PLANE, tok, width), bf16),
            pltpu.VMEM((PLANE, tok, width), bf16),
            pltpu.VMEM((PLANE, dp_count * wrows, model // PLANE), bf16),
            pltpu.VMEM((PLANE, tok, model), bf16),
            pltpu.VMEM((tok, width), bf16),
            pltpu.VMEM((width // HEAD, PLANE, tok, tok), f32),
            pltpu.VMEM((width // HEAD, PLANE, HEAD, tok), bf16),
            pltpu.VMEM((PLANE, dp_count * piece, tok), bf16),
            pltpu.VMEM((PLANE, dp_count * piece, tok), bf16),
            pltpu.VMEM((dp_count, piece, model), f32),
            pltpu.VMEM((CHUNKS, dp_count, 2 * piece, part // 2), bf16),
            pltpu.VMEM((CHUNKS, dp_count - 1, 2 * piece, part // 2), bf16),
            pltpu.VMEM((PLANE, tok, model // PLANE), f32),
            pltpu.VMEM((PLANE, tok // 2, model // PLANE), bf16),
            pltpu.VMEM((PLANE, tok // 2, model // PLANE), bf16),
            pltpu.VMEM((1, model), f32),
            pltpu.SemaphoreType.DMA((5 + PLANE,)),
            pltpu.SemaphoreType.DMA((copies,)),
            pltpu.SemaphoreType.DMA((copies,)),
        ],
        compiler_params=pltpu.CompilerParams(
            collective_id=0, has_side_effects=True, vmem_limit_bytes=62 * 2**20),
    )(queries[0], keys[0], values[0], proj_weight[0], gate_table, timestep, span_index, cotangent[0])
    return output[None], grad.reshape(1, -1, 128)


def local(queries, keys, values, proj_weight, gate_table, timestep, span_index, cotangent):
    tok_rows = queries.shape[1]
    width = queries.shape[2]
    heads_here = width // HEAD
    inv_root = HEAD ** (-0.5)
    seq_place = lax.axis_index("seq")
    all_keys, all_values = (
        lax.all_gather(keys[0], "seq", axis=0, tiled=True),
        lax.all_gather(values[0], "seq", axis=0, tiled=True),
    )
    key_count = all_keys.shape[0]
    query_heads = queries[0].reshape(tok_rows, heads_here, HEAD)
    key_heads = all_keys.reshape(key_count, heads_here, HEAD)
    value_heads = all_values.reshape(key_count, heads_here, HEAD)
    scores = (
        jnp.einsum("qhd,khd->hqk", query_heads, key_heads, preferred_element_type=jnp.float32)
        * inv_root
    )
    key_span = jnp.arange(key_count, dtype=jnp.int32) // tok_rows
    visible = key_span <= jnp.minimum(seq_place, span_index[0])
    scores = jnp.where(visible[None, None, :], scores, -jnp.inf)
    row_top = jnp.max(scores, axis=2, keepdims=True)
    weights = jnp.exp(scores - row_top)
    probs = (weights / jnp.sum(weights, axis=2, keepdims=True)).astype(jnp.bfloat16)
    attended = jnp.einsum("hqk,khd->qhd", probs, value_heads, preferred_element_type=jnp.float32)
    attended = attended.reshape(tok_rows, width).astype(jnp.bfloat16)
    weight_rows = lax.all_gather(proj_weight, "dp", axis=1, tiled=True)
    mixed = jnp.dot(attended, weight_rows[0], preferred_element_type=jnp.float32)
    shared = lax.psum_scatter(
        mixed.astype(jnp.bfloat16), "mp", scatter_dimension=0, tiled=True
    ).astype(jnp.float32)
    step_hit = jnp.arange(gate_table.shape[0], dtype=jnp.int32) == timestep[0]
    gate = jnp.sum(jnp.where(step_hit[:, None], gate_table, 0.0), axis=0)
    output = (gate[None, :] * shared).astype(jnp.bfloat16)[None]
    scaled = (gate[None, :] * cotangent[0].astype(jnp.float32)).astype(jnp.bfloat16)
    term = jnp.dot(attended.T, scaled, preferred_element_type=jnp.float32).reshape(-1, 128)
    rows_all = term.shape[0]
    dp_count = lax.axis_size("dp")
    seq_count = lax.axis_size("seq")
    block_rows = rows_all // (dp_count * seq_count)
    grid_view = term.reshape(dp_count, seq_count, block_rows, 128)
    local_sum = lax.psum_scatter(
        grid_view.transpose(1, 0, 2, 3)
        .reshape(lax.axis_size("seq") * (rows_all // seq_count), 128)
        .astype(jnp.bfloat16),
        "seq",
        scatter_dimension=0,
        tiled=True,
    ).astype(jnp.float32)
    piece = lax.psum_scatter(local_sum, "dp", scatter_dimension=0, tiled=True)
    return (output, piece[None])


def solution(mesh):
    small = mesh.shape["seq"] == PLANE and mesh.shape["mp"] == 2 and mesh.shape["dp"] == 4
    return jax.shard_map(
        functools.partial(fused_local, mesh.shape["dp"]) if small else local,
        mesh=mesh,
        in_specs=(
            P("dp", "seq", "mp"),
            P("dp", "seq", "mp"),
            P("dp", "seq", "mp"),
            P("mp", "dp", None),
            P(),
            P("dp"),
            P("dp"),
            P("dp", "seq", None),
        ),
        out_specs=(P("dp", ("seq", "mp"), None), P("mp", ("dp", "seq"), None)),
        check_vma=False,
    )
```
